512 devices in a mesh: group: 8 (over y_lo, x), member: 64 (over z, y_hi, core).
Axes of the slice: x: 4, y: 4 (y_hi: 2, y_lo: 2; y = y_hi * 2 + y_lo), z: 16, core: 2. Of those that a mesh axis runs over, the one named last changes fastest.
Arguments:
- grads: bfloat16 [1, 131072, 1024], P(None, ('group', 'member')), may hold values from -3000 to 3000
- member_partner: int32 [64], replicated, may hold values from 0 to 63, as said below
- group_partner: int32 [512], replicated, may hold values from 0 to 511, as said below
Outputs:
- tiles: float32 [2, 131072, 256], P(None, ('group', 'member'))
- self_scores: float32 [131072], P(('group', 'member'))
The draws below stay inside these ranges and needn't reach their ends.
Inputs may be any that keep to these rules, and one draw needn't show every extreme that they name: Pairs the blocks of a group: member_partner[member_partner[m]] == m and member_partner[m] != m. Pairs the blocks: group_partner[group_partner[b]] == b; all blocks of group g are paired with blocks of one other group, the same for all of g's blocks, each block of that group once.
All inputs are finite; a program needn't handle non-finite values.
Results may differ from the reference program's by a relative error of at most 0.0047.
Values may be sent and summed in bfloat16 or wider, within the bound.
A program may use at most 128 MiB of HBM per device.

```python
import math
import jax
import jax.numpy as jnp
from jax import lax

K = 1024
LAYERS = 1
ROWS_DEV = 256
MEMBERS = 64
GROUPS = 8
BLOCKS = 512
ROWS = 131072
N_GROUP = 8
N_MEMBER = 64


def pairing(key, count):
    order = jax.random.permutation(key, count).astype(jnp.int32)
    first = order[0::2]
    second = order[1::2]
    partner = jnp.zeros((count,), jnp.int32)
    partner = partner.at[first].set(second)
    partner = partner.at[second].set(first)
    return partner


def draw_member_partner(key, part):
    key = jax.random.fold_in(key, 11)
    return pairing(key, MEMBERS)


def draw_group_partner(key, part):
    key = jax.random.fold_in(key, 23)
    keys = jax.random.split(key, 2)
    order = jax.random.permutation(keys[0], GROUPS).astype(jnp.int32)
    first = order[0::2]
    second = order[1::2]
    pair_keys = jax.random.split(keys[1], GROUPS // 2)
    matching = jax.vmap(lambda one: jax.random.permutation(one, MEMBERS).astype(jnp.int32))(pair_keys)
    steps_member = jnp.arange(MEMBERS, dtype=jnp.int32)
    sources = (first[:, None] * MEMBERS + steps_member[None, :]).reshape(-1)
    targets = (second[:, None] * MEMBERS + matching).reshape(-1)
    partner = jnp.zeros((BLOCKS,), jnp.int32)
    partner = partner.at[sources].set(targets)
    partner = partner.at[targets].set(sources)
    return partner


def draw_grads(key, part):
    key = jax.random.fold_in(key, 5)
    keys = jax.random.split(key, 3)
    shape = (LAYERS, ROWS, K)
    columns = jnp.exp(jax.random.uniform(keys[1], (K,), jnp.float32, 0.0, math.log(10.0)))
    rising = jnp.exp(math.log(3.0) * jnp.arange(ROWS, dtype=jnp.float32) / (ROWS - 1))
    base = jax.random.normal(keys[0], shape, jnp.float32)
    row_scale = jnp.exp(jax.random.uniform(keys[2], (LAYERS, ROWS, 1), jnp.float32, math.log(0.5), math.log(5.0)))
    mixed = base + 0.5 * jnp.roll(base, -1, axis=2) + 0.3 * jnp.roll(base, -37, axis=2)
    value = mixed * columns[None, None, :] * row_scale * rising[None, :, None]
    return value.astype(jnp.bfloat16)


def setup_inputs(seed: int = 0) -> dict:
    arg_keys = jax.random.split(jax.random.key(seed), 4)
    grads = draw_grads(jax.random.fold_in(arg_keys[3], 71), 0)
    member_partner = draw_member_partner(jax.random.fold_in(arg_keys[3], 71), 0)
    group_partner = draw_group_partner(jax.random.fold_in(arg_keys[3], 71), 0)
    return dict(grads=grads, member_partner=member_partner, group_partner=group_partner)


DAMP = 1.0

def precondition(block, chol):
    right = block.astype(jnp.float32).T
    half = jax.scipy.linalg.solve_triangular(chol, right, lower=True)
    whole = jax.scipy.linalg.solve_triangular(chol, half, lower=True, trans=1)
    return whole.T.astype(jnp.bfloat16)

def reference(grads, member_partner, group_partner):
    rows_all = grads.shape[1]
    eye = jnp.eye(K, dtype=jnp.float32)
    precond_list = []
    for layer in range(LAYERS):
        block = grads[layer]
        fisher = lax.dot_general(block.astype(jnp.float32), block.astype(jnp.float32), (((0,), (0,)), ((), ())), preferred_element_type=jnp.float32)
        fisher = fisher / rows_all + DAMP * eye
        chol = jnp.linalg.cholesky(fisher)
        precond_list.append(precondition(block, chol))
    precond = jnp.stack(precond_list)
    self_scores = lax.optimization_barrier(jnp.sum(precond.astype(jnp.float32) * grads.astype(jnp.float32), axis=(0, 2))) / (LAYERS * K)
    blocks = N_GROUP * N_MEMBER
    scale = 1.0 / math.sqrt(LAYERS * K)
    index = jnp.arange(blocks, dtype=jnp.int32)
    group_of = index // N_MEMBER
    member_of = index % N_MEMBER
    partners = [group_of * N_MEMBER + member_partner[member_of], group_partner[index].astype(jnp.int32)]
    precond_blocks = precond.reshape(LAYERS, blocks, ROWS_DEV, K)
    grad_blocks = grads.reshape(LAYERS, blocks, ROWS_DEV, K)

    def tile_of(item):
        own, other, below = item
        left = jnp.where(below, precond_blocks[:, own], grad_blocks[:, own])
        right = jnp.where(below, grad_blocks[:, other], precond_blocks[:, other])
        product = jnp.einsum('lrk,lsk->rs', left.astype(jnp.float32), right.astype(jnp.float32), precision=lax.Precision.HIGHEST)
        return product * scale
    rounds = []
    for partner in partners:
        below = index < partner
        tiles_round = lax.map(tile_of, (index, partner.astype(jnp.int32), below))
        rounds.append(tiles_round.reshape(blocks * ROWS_DEV, ROWS_DEV))
    tiles = jnp.stack(rounds)
    return (tiles, self_scores)
```

```python
import functools
import math

import jax
import jax.numpy as jnp
from jax import lax
from jax.experimental import pallas as pl
from jax.experimental.pallas import tpu as pltpu
from jax.sharding import PartitionSpec as P

HI = lax.Precision.HIGHEST
NB = 8
B = 128

def dot(a, b, dims, precision=None):
    return lax.dot_general(a, b, (dims, ((), ())), precision=precision, preferred_element_type=jnp.float32)

def invert128(block):
    lane = lax.broadcasted_iota(jnp.int32, (8, B), 1)
    sub = lax.broadcasted_iota(jnp.int32, (8, B), 0)
    low = lane < 8
    unit = jnp.where(lane == sub, 1.0, 0.0).astype(jnp.float32)
    full = lambda v: jnp.broadcast_to(v, (8, B))
    rows = tuple(block[8 * i : 8 * i + 8] for i in range(16))
    first = tuple(full(rows[0][:, c : c + 1]) for c in range(8))

    def step(_, carry):
        a, cols = carry[:16], list(carry[16:])
        work = jnp.where(low, unit, a[0])
        for p in range(8):
            here = sub == p
            r = 1.0 / full(cols[p][p : p + 1])
            m = jnp.where(here, -r, cols[p] * r)
            for c in range(p + 1, 8):
                cols[c] = jnp.where(here, 0.0, cols[c]) - m * full(cols[c][p : p + 1])
            work = jnp.where(here, 0.0, work) - m * full(work[p : p + 1])
        wrow = [full(work[c : c + 1]) for c in range(8)]
        new = []
        for i in range(1, 16):
            t = [full(a[i][:, c : c + 1]) * wrow[c] for c in range(8)]
            s = ((t[0] + t[1]) + (t[2] + t[3])) + ((t[4] + t[5]) + (t[6] + t[7]))
            new.append(jnp.where(low, 0.0, a[i]) - s)
        new.append(work)
        nxt = tuple(full(new[0][:, 8 + c : 9 + c]) for c in range(8))
        return tuple(pltpu.roll(v, B - 8, 1) for v in new) + nxt

    out = lax.fori_loop(0, 16, step, rows + first)
    return jnp.concatenate(out[:16], axis=0)

def off(j):
    return sum((NB - t) * B for t in range(j))

def offg(j):
    return sum((NB - t) * B + 256 for t in range(j))

def kernel(below_ref, f_ref, g_ref, p0_ref, p1_ref, tiles_ref, scores_ref, a_ref, m_ref, x_ref, *, rows_all):
    eye = (lax.broadcasted_iota(jnp.int32, (B, B), 0) == lax.broadcasted_iota(jnp.int32, (B, B), 1)).astype(jnp.float32)
    for j in range(NB):
        n = (NB - j) * B
        a_ref[offg(j) : offg(j) + n] = f_ref[off(j) : off(j) + n] * (1.0 / rows_all)
        a_ref[offg(j) : offg(j) + B] += eye
        a_ref[offg(j) + n : offg(j) + n + 256] = g_ref[:, j * B : (j + 1) * B].astype(jnp.float32)
    for j in range(NB):
        o, n = offg(j), (NB - j) * B + 256
        inv = invert128(a_ref[o : o + B])
        m_ref[o + B : o + n] = dot(a_ref[o + B : o + n], inv, ((1,), (0,)), HI)
        for t in range(j + 1, NB):
            ot, nt = offg(t), (NB - t) * B + 256
            a_ref[ot : ot + nt] -= dot(m_ref[o + n - nt : o + n], a_ref[o + (t - j) * B : o + (t - j + 1) * B], ((1,), (1,)), HI)
    for j in reversed(range(NB)):
        o, n = offg(j), (NB - j) * B + 256
        z = m_ref[o + n - 256 : o + n]
        if j < NB - 1:
            z = z - dot(x_ref[:, (j + 1) * B :], m_ref[o + B : o + n - 256], ((1,), (0,)), HI)
        x_ref[:, j * B : (j + 1) * B] = z
    x = x_ref[...]
    hi = x.astype(jnp.bfloat16)
    lo = (x - hi.astype(jnp.float32)).astype(jnp.bfloat16)
    prod = hi.astype(jnp.float32) * g_ref[...].astype(jnp.float32)
    part = sum(prod[:, j * B : (j + 1) * B] for j in range(NB))
    scores_ref[...] = jnp.sum(part.T, axis=0, keepdims=True) * (1.0 / (NB * B))
    scale = 1.0 / math.sqrt(NB * B)
    for r, other in enumerate((p0_ref, p1_ref)):
        rest = jnp.where(below_ref[r] != 0, jnp.zeros_like(lo), lo)
        tiles_ref[r] = (dot(hi, other[...], ((1,), (1,))) + dot(rest, other[...], ((1,), (1,)))) * scale

def finish(below, f, g, p0, p1, rows_all):
    vm = pl.BlockSpec(memory_space=pltpu.VMEM)
    return pl.pallas_call(
        functools.partial(kernel, rows_all=rows_all),
        out_shape=(jax.ShapeDtypeStruct((2, 256, 256), jnp.float32), jax.ShapeDtypeStruct((1, 256), jnp.float32)),
        in_specs=[pl.BlockSpec(memory_space=pltpu.SMEM), vm, vm, vm, vm],
        out_specs=(vm, vm),
        scratch_shapes=[
            pltpu.VMEM((offg(NB), B), jnp.float32),
            pltpu.VMEM((offg(NB), B), jnp.float32),
            pltpu.VMEM((256, NB * B), jnp.float32),
        ],
        compiler_params=pltpu.CompilerParams(vmem_limit_bytes=48 << 20),
    )(below, f, g, p0, p1)


MESH = pl.DeviceIdType.MESH
TOTAL = NB * (NB + 1) // 2 * B
HALF = TOTAL // 2
PLANE = 16
SHARD = HALF // PLANE
DEPTH = 16
UNIT = 16
OWNERS = SHARD // UNIT


def place(x, y, z, core):
    return (lax.rem(y, 2) * 4 + x, z * 4 + lax.div(y, 2) * 2 + core)


def reduce_kernel(g_ref, f_ref, v_ref, gt_ref, s1, r1, s2, r2, w_ref, r3,
                  s1_sem, r1_sem, s2_sem, r2_sem, s3_sem, r3_sem, s4_sem, r4_sem, s5_sem, r5_sem, s6_sem, r6_sem):
    group, member = lax.axis_index("group"), lax.axis_index("member")
    x, y = lax.rem(group, 4), lax.div(group, 4) + 2 * lax.rem(lax.div(member, 2), 2)
    z, core = lax.div(member, 4), lax.rem(member, 2)
    spot = x * 4 + y

    def in_plane(s):
        return place(lax.div(s, 4), lax.rem(s, 4), z, core)

    def peer(k):
        return lax.rem(spot + k, PLANE)

    def on_column(other):
        return place(x, y, other, core)

    twin = place(x, y, z, 1 - core)

    def send(src, dst, ssem, rsem, dev):
        return pltpu.make_async_remote_copy(
            src_ref=src, dst_ref=dst, send_sem=ssem, recv_sem=rsem, device_id=dev, device_id_type=MESH
        )

    barrier = pltpu.get_barrier_semaphore()
    pl.semaphore_signal(barrier, inc=1, device_id=twin, device_id_type=MESH)
    for k in range(1, PLANE):
        pl.semaphore_signal(barrier, inc=1, device_id=in_plane(peer(k)), device_id_type=MESH)
    for k in range(1, DEPTH):
        pl.semaphore_signal(barrier, inc=1, device_id=on_column(lax.rem(z + k, DEPTH)), device_id_type=MESH)

    gt_ref[...] = g_ref[...].T
    for j in range(NB):
        v_ref[off(j) : off(j + 1)] = dot(gt_ref[j * B :], g_ref[:, j * B : (j + 1) * B], ((1,), (0,)))
    mine = pl.multiple_of(core * HALF, SHARD)
    theirs = pl.multiple_of((1 - core) * HALF, SHARD)
    s1[...] = v_ref[pl.ds(theirs, HALF)].astype(jnp.bfloat16)
    pl.semaphore_wait(barrier, PLANE + DEPTH - 1)

    c1 = send(s1, r1, s1_sem, r1_sem, twin)
    c1.start()
    c1.wait_recv()

    def shard(s):
        return pl.multiple_of(s * SHARD, SHARD)

    c2 = []
    for k in range(1, PLANE):
        s = peer(k)
        s2[k] = (v_ref[pl.ds(mine + shard(s), SHARD)] + r1[pl.ds(shard(s), SHARD)].astype(jnp.float32)).astype(jnp.bfloat16)
        c2.append(send(s2.at[k], r2.at[k], s2_sem.at[k], r2_sem.at[k], in_plane(s)))
        c2[-1].start()
    total = v_ref[pl.ds(mine + shard(spot), SHARD)] + r1[pl.ds(shard(spot), SHARD)].astype(jnp.float32)
    for k in range(1, PLANE):
        c2[k - 1].wait_recv()
        total += r2[k].astype(jnp.float32)
    w_ref[...] = total

    here = mine + shard(spot)

    def c3(u):
        k = lax.rem(u - z + DEPTH, DEPTH)
        return send(w_ref.at[pl.ds(u * UNIT, UNIT)], r3.at[k], s3_sem.at[u], r3_sem.at[k], on_column(u))

    def out_rows(u):
        return f_ref.at[pl.ds(pl.multiple_of(here + u * UNIT, UNIT), UNIT)]

    for u in range(OWNERS):
        @pl.when(z != u)
        def _(u=u):
            c3(u).start()

    @pl.when(z < OWNERS)
    def _():
        unit = w_ref[pl.ds(pl.multiple_of(z * UNIT, UNIT), UNIT)]
        for k in range(1, DEPTH):
            send(w_ref.at[pl.ds(0, UNIT)], r3.at[k], s3_sem.at[0], r3_sem.at[k], twin).wait_recv()
            unit += r3[k]
        f_ref[pl.ds(pl.multiple_of(here + z * UNIT, UNIT), UNIT)] = unit
        for k in range(1, DEPTH):
            send(out_rows(z), out_rows(z), s4_sem.at[k], r4_sem.at[z], on_column(lax.rem(z + k, DEPTH))).start()

    for u in range(OWNERS):
        @pl.when(z != u)
        def _(u=u):
            send(out_rows(u), out_rows(u), s4_sem.at[0], r4_sem.at[u], twin).wait_recv()

    def rows_of(s, half):
        return f_ref.at[pl.ds(pl.multiple_of(half + shard(s), SHARD), SHARD)]

    c6 = [send(rows_of(spot, mine), rows_of(spot, mine), s6_sem.at[0], r6_sem.at[0], twin)]
    c6[0].start()
    c5 = []
    for k in range(1, PLANE):
        c5.append(send(rows_of(spot, mine), rows_of(spot, mine), s5_sem.at[k], r5_sem.at[k], in_plane(peer(k))))
        c5[-1].start()
    for k in range(1, PLANE):
        s = peer(PLANE - k)
        send(rows_of(s, mine), rows_of(s, mine), s5_sem.at[k], r5_sem.at[k], twin).wait_recv()
        c6.append(send(rows_of(s, mine), rows_of(s, mine), s6_sem.at[k], r6_sem.at[k], twin))
        c6[-1].start()
    for k in range(PLANE):
        s = peer(PLANE - k)
        send(rows_of(s, theirs), rows_of(s, theirs), s6_sem.at[k], r6_sem.at[k], twin).wait_recv()

    c1.wait_send()
    for c in c2 + c5 + c6:
        c.wait_send()
    for u in range(OWNERS):
        @pl.when(z != u)
        def _(u=u):
            c3(u).wait_send()

    @pl.when(z < OWNERS)
    def _():
        for k in range(1, DEPTH):
            send(out_rows(z), out_rows(z), s4_sem.at[k], r4_sem.at[z], twin).wait_send()


def fisher_sum(block):
    vm = pl.BlockSpec(memory_space=pltpu.VMEM)
    sems = lambda *n: pltpu.SemaphoreType.DMA(n)
    return pl.pallas_call(
        reduce_kernel,
        out_shape=jax.ShapeDtypeStruct((TOTAL, B), jnp.float32),
        in_specs=[vm],
        out_specs=vm,
        scratch_shapes=[
            pltpu.VMEM((TOTAL, B), jnp.float32),
            pltpu.VMEM((NB * B, 256), jnp.bfloat16),
            pltpu.VMEM((HALF, B), jnp.bfloat16),
            pltpu.VMEM((HALF, B), jnp.bfloat16),
            pltpu.VMEM((PLANE, SHARD, B), jnp.bfloat16),
            pltpu.VMEM((PLANE, SHARD, B), jnp.bfloat16),
            pltpu.VMEM((SHARD, B), jnp.float32),
            pltpu.VMEM((DEPTH, UNIT, B), jnp.float32),
            pltpu.SemaphoreType.DMA, pltpu.SemaphoreType.DMA,
            sems(PLANE), sems(PLANE), sems(DEPTH), sems(DEPTH), sems(DEPTH), sems(DEPTH),
            sems(PLANE), sems(PLANE), sems(PLANE), sems(PLANE),
        ],
        compiler_params=pltpu.CompilerParams(collective_id=0, has_side_effects=True, vmem_limit_bytes=48 << 20),
    )(block)


def exchange(block, member_partner, group_partner):
    rows, width = block.shape
    members, groups = lax.axis_size("member"), lax.axis_size("group")
    group_here = lax.axis_index("group")
    partner_groups = group_partner[jnp.arange(groups, dtype=jnp.int32) * members] // members
    other_group = partner_groups[group_here]
    source_members = (
        lax.dynamic_slice(group_partner, (group_here * members,), (members,)) % members
    )
    spread = lax.all_to_all(
        block.reshape(members, rows // members, width), "member", split_axis=0, concat_axis=0, tiled=True
    )
    first = lax.all_to_all(
        jnp.take(spread, member_partner, axis=0), "member", split_axis=0, concat_axis=0, tiled=True
    ).reshape(rows, width)
    pieces = spread.reshape(groups, rows // groups, width)
    pieces = lax.all_to_all(pieces, "group", split_axis=0, concat_axis=0, tiled=True)
    pieces = lax.all_to_all(
        jnp.take(pieces, partner_groups, axis=0), "group", split_axis=0, concat_axis=0, tiled=True
    ).reshape(members, rows // members, width)
    second = lax.all_to_all(
        jnp.take(pieces, source_members, axis=0), "member", split_axis=0, concat_axis=0, tiled=True
    ).reshape(rows, width)
    return first, second


def per_device(grads, member_partner, group_partner):
    block = grads[0]
    rows_all = block.shape[0] * lax.axis_size("member") * lax.axis_size("group")
    member_here = lax.axis_index("member")
    block_here = lax.axis_index("group") * lax.axis_size("member") + member_here
    below = jnp.stack(
        [member_here < member_partner[member_here], block_here < group_partner[block_here]]
    ).astype(jnp.int32)
    first, second = exchange(block, member_partner, group_partner)
    fisher = fisher_sum(block)
    tiles, scores = finish(below, fisher, block, first, second, rows_all)
    return (tiles, scores.reshape(-1))


def solution(mesh):
    return jax.shard_map(
        per_device,
        mesh=mesh,
        in_specs=(P(None, ("group", "member"), None), P(), P()),
        out_specs=(P(None, ("group", "member"), None), P(("group", "member"))),
        check_vma=False,
    )
```
